256 devices in a mesh: row: 32 (over z_hi, y, core), col: 8 (over x, z_lo).
Axes of the slice: x: 4, y: 4, z: 8 (z_hi: 4, z_lo: 2; z = z_hi * 2 + z_lo), core: 2. Of those that a mesh axis runs over, the one named last changes fastest.
Arguments:
- blocks: bfloat16 [32, 8, 16, 128, 128], P('row', 'col'), may hold values from -1.5 to 1.5
- slot_rows: int32 [32, 8, 16], P('row', 'col'), may hold values from 0 to 19, as said below
- slot_cols: int32 [32, 8, 16], P('row', 'col'), may hold values from 0 to 1
- counts: int32 [32, 8], P('row', 'col'), may hold values from 8 to 16, as said below
- col_window: int32 [8, 2], P('col'), may hold values from 0 to 79
Outputs:
- panel_product: float32 [640, 16, 128, 128], P('row', 'col')
The draws below stay inside these ranges and needn't reach their ends.
Inputs may be any that keep to these rules, and one draw needn't show every extreme that they name: `slot_rows`: within one device, the live slots name distinct positions. `counts`: 16 is reached on some device.
All inputs are finite; a program needn't handle non-finite values.
Results may differ from the reference program's by a relative error of at most 0.0003.
Values may be sent and summed in bfloat16 or wider, within the bound.
A program may use at most 128 MiB of HBM per device.

```python
import jax
import jax.numpy as jnp
from jax import lax

BLK = 128
KP = 16
RL = 20
CL = 2
P_SIZE = 16
KPC = 2
GROUP = 4
WIN_ROWS = 640
N_ROW = 32
N_COL = 8


def slot_positions(key):
    base_key = jax.random.fold_in(key, 11)
    device_keys = jax.random.split(base_key, N_ROW * N_COL)
    chosen = jax.vmap(lambda one_key: jax.random.permutation(one_key, RL * KPC)[:P_SIZE])(device_keys)
    return chosen.reshape(N_ROW, N_COL, P_SIZE).astype(jnp.int32)


def draw_slot_rows(key, part):
    return (slot_positions(key) // KPC).astype(jnp.int32)


def draw_slot_cols(key, part):
    return (slot_positions(key) % KPC).astype(jnp.int32)


def draw_counts(key, part):
    drawn = jax.random.randint(jax.random.fold_in(key, 23), (N_ROW, N_COL), P_SIZE // 2, P_SIZE + 1)
    drawn = drawn.at[0, 0].set(P_SIZE)
    drawn = drawn.at[N_ROW - 1, N_COL - 1].set(P_SIZE // 2)
    return drawn.astype(jnp.int32)


def draw_col_window(key, part):
    drawn = jax.random.randint(jax.random.fold_in(key, 37), (N_COL, CL), 0, GROUP * RL)
    drawn = drawn.at[0, 0].set(GROUP * RL - 1)
    drawn = drawn.at[0, 1].set(0)
    return drawn.astype(jnp.int32)


def steps_of(key, dims, pieces, least, largest):
    loudness, own = 1.0, jax.random.fold_in(key, 6)
    for position, shards_of in pieces:
        steps = jnp.exp(jax.random.uniform(jax.random.fold_in(own, position), (shards_of,), jnp.float32, least / len(pieces), largest / len(pieces)))
        loudness = loudness * jnp.repeat(steps, dims[position] // shards_of).reshape([-1 if axis == position else 1 for axis in range(len(dims))])
    return loudness


def noise(stream_key, shape, scale, bound, cuts=(), dtype=jnp.bfloat16):
    array = jax.random.normal(stream_key, shape, jnp.float32) * scale
    if len(cuts) > 0:
        array = steps_of(stream_key, shape, cuts, -0.22, 0.18) * array
    return jnp.clip(array, min=-bound, max=bound).astype(dtype)


def setup_inputs(seed: int = 0) -> dict:
    arg_keys = jax.random.split(jax.random.key(seed), 6)
    blocks = noise(arg_keys[0], (N_ROW, N_COL, P_SIZE, BLK, BLK), 0.25, 1.5, ((0, 32), (1, 8)))
    slot_rows = draw_slot_rows(jax.random.fold_in(arg_keys[5], 71), 0)
    slot_cols = draw_slot_cols(jax.random.fold_in(arg_keys[5], 71), 0)
    counts = draw_counts(jax.random.fold_in(arg_keys[5], 71), 0)
    col_window = draw_col_window(jax.random.fold_in(arg_keys[5], 71), 0)
    return dict(blocks=blocks, slot_rows=slot_rows, slot_cols=slot_cols, counts=counts, col_window=col_window)


def reference(blocks, slot_rows, slot_cols, counts, col_window):
    live_slots = jnp.arange(P_SIZE)[None, None, :] < counts[:, :, None]
    row_owner = jnp.broadcast_to(jnp.arange(N_ROW)[:, None, None], slot_rows.shape)
    col_owner = jnp.broadcast_to(jnp.arange(N_COL)[None, :, None], slot_rows.shape)
    kept = jnp.where(live_slots[..., None, None], blocks.astype(jnp.float32), jnp.float32(0.0))
    dense = jnp.zeros((N_ROW, RL, N_COL, KPC, BLK, BLK), jnp.float32)
    dense = dense.at[row_owner, slot_rows, col_owner, slot_cols].add(kept)
    panel_blocks = dense.transpose(0, 1, 4, 2, 3, 5).reshape(WIN_ROWS, BLK, KP * BLK).astype(jnp.bfloat16)
    partner = (jnp.arange(N_COL)[:, None] * (GROUP * RL) + col_window).reshape(-1)
    right_side = panel_blocks[partner].astype(jnp.float32)

    def one_row(left_strip):
        return jnp.einsum("xk,nyk->nxy", left_strip.astype(jnp.float32), right_side, precision=lax.Precision.HIGHEST)

    return lax.map(one_row, panel_blocks)
```

```python
import jax
import jax.numpy as jnp
from jax import lax
from jax.experimental import pallas as pl
from jax.experimental.pallas import tpu as pltpu
from jax.sharding import PartitionSpec as P

MESH = pl.DeviceIdType.MESH
BLK = 128
RL = 20
SLOTS = 16
NONE = SLOTS
COLS = 8
WINDOW_LANE = 64

CHUNKS = {"ZA": (0, 5), "ZB": (5, 5), "XA": (10, 3), "XB": (13, 3)}
SOURCES = ((0, 0), (0, 1), (-1, 0), (1, 0), (2, 0), (-1, 1), (1, 1), (2, 1))
ROWS_AT_ONCE = 5


def kernel(
    blocks_ref, rows_ref, cols_ref, counts_ref, window_ref, out_ref,
    own, store_1, store_2, store_3, store_4, store_5, store_6, store_7,
    meta, table, picked, offered, right,
    left_send, left_recv, meta_send, meta_recv, offer_send, offer_recv, spread_send, spread_recv, local_sem,
):
    r = lax.axis_index("row")
    c = lax.axis_index("col")
    zh, y, k = r // 8, lax.rem(r // 2, 4), lax.rem(r, 2)
    x, zl = c // 2, lax.rem(c, 2)
    store = dict(zip(SOURCES, (own, store_1, store_2, store_3, store_4, store_5, store_6, store_7)))

    def column_of(dx, dz):
        return lax.rem(x + (dx + 4), 4) * 2 + (zl if dz == 0 else 1 - zl)

    to_right, to_left, to_pair = column_of(1, 0), column_of(-1, 0), column_of(0, 1)
    target, part = r // 4, lax.rem(r, 4)
    offer_rows = [4 * lax.rem(c + 1, COLS) + t for t in range(4)]
    offering = lax.rem(r // 4 + (COLS - 1), COLS)

    load_own = pltpu.make_async_copy(blocks_ref.at[0, 0], own.at[pl.ds(0, SLOTS)], local_sem.at[0])
    load_own.start()

    barrier = pltpu.get_barrier_semaphore()
    senders = [(r, lax.rem(c + o, COLS)) for o in range(1, COLS)]
    senders += [(4 * c + g, offering) for g in range(4)]
    senders += [(lax.rem(zh + o, 4) * 8 + y * 2 + k, c) for o in range(1, 4)]
    senders += [(zh * 8 + lax.rem(y + o, 4) * 2 + k, c) for o in range(1, 4)]
    senders += [(zh * 8 + y * 2 + 1 - k, c)]
    for sender in senders:
        pl.semaphore_signal(barrier, inc=1, device_id=sender, device_id_type=MESH)

    lane = lax.broadcasted_iota(jnp.int32, (8, 128), 1)
    found = jnp.full((8, 128), NONE, jnp.int32)
    live = counts_ref[0, 0]
    for s in range(SLOTS):
        position = jnp.where(s < live, rows_ref[0, 0, s] * 2 + cols_ref[0, 0, s], 127)
        found = jnp.where(lane == position, s, found)
    for b in range(2):
        found = jnp.where(lane == WINDOW_LANE + b, window_ref[0, b], found)
    meta[0] = found
    for source in SOURCES:
        store[source][NONE] = jnp.zeros((BLK, BLK), jnp.bfloat16)

    pl.semaphore_wait(barrier, len(senders))

    started = []

    def send(src, dst, send_sem, recv_sem, device):
        copy = pltpu.make_async_remote_copy(
            src_ref=src, dst_ref=dst, send_sem=send_sem, recv_sem=recv_sem, device_id=device, device_id_type=MESH
        )
        copy.start()
        started.append(copy)
        return copy

    left = {}

    def send_left(source, chunk, column, lands):
        first, size = CHUNKS[chunk]
        sem = len(left)
        left[(lands, chunk)] = send(
            store[source].at[pl.ds(first, size)], store[lands].at[pl.ds(first, size)],
            left_send.at[sem], left_recv.at[sem], (r, column),
        )

    meta_copies = [
        send(meta.at[0], meta.at[o], meta_send.at[o], meta_recv.at[o], (r, lax.rem(c + o, COLS)))
        for o in range(1, COLS)
    ]
    load_own.wait()
    send_left((0, 0), "ZA", to_pair, (0, 1))
    send_left((0, 0), "XA", to_right, (-1, 0))
    send_left((0, 0), "XB", to_left, (1, 0))
    send_left((0, 0), "XB", to_right, (-1, 0))
    send_left((0, 0), "XA", to_left, (1, 0))

    for copy in meta_copies:
        copy.wait_recv()
    load_table = pltpu.make_async_copy(meta, table, local_sem.at[1])
    load_table.start()
    load_table.wait()

    window_source = lax.rem(c - target + COLS, COLS)
    for b in range(2):
        row = table[window_source, 0, WINDOW_LANE + b] - part * RL
        mine = (row >= 0) & (row < RL)
        for j in range(2):
            place = jnp.where(mine, row, 0) * 2 + j
            slot = jnp.where(mine, table[0, 0, place], NONE)
            picked[2 * b + j] = own[slot]
    for t in range(4):
        send(picked.at[t], offered.at[part], offer_send.at[t], offer_recv.at[part], (offer_rows[t], target))

    send_left((0, 0), "ZB", to_pair, (0, 1))
    send_left((0, 0), "ZA", to_right, (-1, 0))
    send_left((0, 0), "ZB", to_left, (1, 0))
    send_left((0, 0), "ZB", to_right, (-1, 0))
    send_left((0, 0), "ZA", to_left, (1, 0))
    send_left((0, 0), "XA", to_pair, (0, 1))
    send_left((0, 0), "XB", to_pair, (0, 1))

    def arrived(lands, *chunks):
        for chunk in chunks:
            left[(lands, chunk)].wait_recv()

    for g in range(4):
        pltpu.make_async_remote_copy(
            src_ref=picked.at[g], dst_ref=offered.at[g], send_sem=offer_send.at[g], recv_sem=offer_recv.at[g],
            device_id=(offer_rows[0], target), device_id_type=MESH,
        ).wait_recv()
    total = offered[0].astype(jnp.float32)
    for g in range(1, 4):
        total = total + offered[g].astype(jnp.float32)
    lane_yk = y * 2 + k
    right[lane_yk, zh] = total.astype(jnp.bfloat16)
    z_copies = [
        send(
            right.at[lane_yk, zh], right.at[lane_yk, zh], spread_send.at[o], spread_recv.at[o],
            (lax.rem(zh + o, 4) * 8 + y * 2 + k, c),
        )
        for o in range(1, 4)
    ]

    arrived((-1, 0), "XA")
    send_left((-1, 0), "XA", to_right, (2, 0))
    arrived((1, 0), "XB")
    send_left((1, 0), "XB", to_left, (2, 0))
    send_left((-1, 0), "XA", to_pair, (-1, 1))
    send_left((1, 0), "XB", to_pair, (1, 1))
    arrived((0, 1), "ZA")
    send_left((0, 1), "ZA", to_right, (-1, 1))
    send_left((0, 1), "ZA", to_left, (1, 1))

    for copy in z_copies:
        copy.wait_recv()
    y_copies = [
        send(
            right.at[lane_yk], right.at[lane_yk], spread_send.at[4 + o], spread_recv.at[4 + o],
            (zh * 8 + lax.rem(y + o, 4) * 2 + k, c),
        )
        for o in range(1, 4)
    ]

    def send_core(o):
        slab = lax.rem(y + (4 - o), 4) * 2 + k
        return send(
            right.at[slab], right.at[slab], spread_send.at[8 + o], spread_recv.at[8 + o], (zh * 8 + y * 2 + 1 - k, c)
        )

    core_copies = [send_core(0)]

    arrived((-1, 0), "XB")
    send_left((-1, 0), "XB", to_pair, (-1, 1))
    arrived((1, 0), "XA")
    send_left((1, 0), "XA", to_pair, (1, 1))
    arrived((0, 1), "ZB")
    send_left((0, 1), "ZB", to_left, (1, 1))
    send_left((0, 1), "ZB", to_right, (-1, 1))
    arrived((-1, 0), "ZA")
    send_left((-1, 0), "ZA", to_right, (2, 0))
    arrived((1, 0), "ZB")
    send_left((1, 0), "ZB", to_left, (2, 0))
    arrived((2, 0), "XA", "XB")
    send_left((2, 0), "XA", to_pair, (2, 1))
    send_left((2, 0), "XB", to_pair, (2, 1))

    for o in (1, 3, 2):
        y_copies[o - 1].wait_recv()
        core_copies.append(send_core(o))

    arrived((-1, 1), "ZA")
    send_left((-1, 1), "ZA", to_right, (2, 1))
    arrived((1, 1), "ZB")
    send_left((1, 1), "ZB", to_left, (2, 1))

    for copy in core_copies:
        copy.wait_recv()

    def multiply(source, first):
        column = column_of(*source)
        entry = lax.rem(c - column + COLS, COLS)
        holder = lax.rem(column + 1, COLS)
        slab, depth = 4 * lax.rem(holder, 2), holder // 2
        factor = jnp.concatenate(
            [
                jnp.concatenate([right[slab + 2 * b + j, depth] for j in range(2)], axis=1)
                for b in range(2)
            ],
            axis=0,
        )

        def some_rows(step, carry):
            strips = []
            for a in range(ROWS_AT_ONCE):
                place = (step * ROWS_AT_ONCE + a) * 2
                strips.append(
                    jnp.concatenate([store[source][table[entry, 0, place + j]] for j in range(2)], axis=1)
                )
            product = lax.dot_general(
                jnp.concatenate(strips, axis=0), factor, (((1,), (1,)), ((), ())), preferred_element_type=jnp.float32
            )
            for a in range(ROWS_AT_ONCE):
                for b in range(2):
                    piece = product[a * BLK:(a + 1) * BLK, b * BLK:(b + 1) * BLK]
                    if first:
                        out_ref[step * ROWS_AT_ONCE + a, b] = piece
                    else:
                        out_ref[step * ROWS_AT_ONCE + a, b] += piece
            return carry

        lax.fori_loop(0, RL // ROWS_AT_ONCE, some_rows, 0)

    waits = {
        (0, 0): (),
        (0, 1): ("XA", "XB"),
        (-1, 0): ("ZB",),
        (1, 0): ("ZA",),
        (2, 0): ("ZA", "ZB"),
        (-1, 1): ("ZB", "XA", "XB"),
        (1, 1): ("ZA", "XA", "XB"),
        (2, 1): ("ZA", "ZB", "XA", "XB"),
    }
    for source in SOURCES:
        arrived(source, *waits[source])
        multiply(source, source == (0, 0))

    for copy in started:
        copy.wait_send()


def per_device(blocks, slot_rows, slot_cols, counts, col_window):
    hbm = pl.BlockSpec(memory_space=pl.ANY)
    scalars = pl.BlockSpec(memory_space=pltpu.SMEM)
    dma = pltpu.SemaphoreType.DMA
    return pl.pallas_call(
        kernel,
        out_shape=jax.ShapeDtypeStruct((RL, 2, BLK, BLK), jnp.float32),
        in_specs=[hbm, scalars, scalars, scalars, scalars],
        out_specs=pl.BlockSpec(memory_space=pltpu.VMEM),
        scratch_shapes=[
            *[pltpu.VMEM((SLOTS + 1, BLK, BLK), jnp.bfloat16) for _ in SOURCES],
            pltpu.VMEM((COLS, 8, 128), jnp.int32),
            pltpu.SMEM((COLS, 8, 128), jnp.int32),
            pltpu.VMEM((4, BLK, BLK), jnp.bfloat16),
            pltpu.VMEM((4, BLK, BLK), jnp.bfloat16),
            pltpu.VMEM((8, 4, BLK, BLK), jnp.bfloat16),
            dma((28,)), dma((28,)), dma((8,)), dma((8,)), dma((4,)), dma((4,)), dma((12,)), dma((12,)), dma((2,)),
        ],
        compiler_params=pltpu.CompilerParams(
            collective_id=0, has_side_effects=True, vmem_limit_bytes=24 * 1024 * 1024
        ),
        cost_estimate=pl.CostEstimate(flops=2 * RL * BLK * 2048 * 256, bytes_accessed=8 * 1024 * 1024, transcendentals=0),
    )(blocks, slot_rows, slot_cols, counts, col_window)


def solution(mesh):
    placed = (
        P("row", "col", None, None, None),
        P("row", "col", None),
        P("row", "col", None),
        P("row", "col"),
        P("col", None),
    )
    return jax.shard_map(
        per_device, mesh=mesh, in_specs=placed, out_specs=P("row", "col", None, None), check_vma=False
    )
```

```python
import jax
import jax.numpy as jnp
from jax import lax
from jax.experimental import pallas as pl
from jax.experimental.pallas import tpu as pltpu
from jax.sharding import PartitionSpec as P

MESH = pl.DeviceIdType.MESH
BLK = 128
RL = 20
SLOTS = 16
NONE = SLOTS
COLS = 8

CHUNKS = {"ZA": (0, 5), "ZB": (5, 5), "XA": (10, 3), "XB": (13, 3)}
SOURCES = ((0, 0), (0, 1), (-1, 0), (1, 0), (2, 0), (-1, 1), (1, 1), (2, 1))


def kernel(
    blocks_ref, rows_ref, cols_ref, window_ref, counts_ref, out_ref,
    own, store_1, store_2, store_3, store_4, store_5, store_6, store_7,
    rows, cols, window, meta, table, own_table, picked, given, mixed, offered, right,
    left_send, left_recv, meta_send, meta_recv, window_send, window_recv, pick_send, pick_recv,
    offer_send, offer_recv, spread_send, spread_recv, local_sem,
):
    r = lax.axis_index("row")
    c = lax.axis_index("col")
    zh, y, k = r // 8, lax.rem(r // 2, 4), lax.rem(r, 2)
    x, zl = c // 2, lax.rem(c, 2)
    store = dict(zip(SOURCES, (own, store_1, store_2, store_3, store_4, store_5, store_6, store_7)))

    def row_of(zh, y, k):
        return zh * 8 + y * 2 + k

    def column_of(dx, dz):
        return lax.rem(x + (dx + 4), 4) * 2 + (zl if dz == 0 else 1 - zl)

    to_right, to_left, to_pair = column_of(1, 0), column_of(-1, 0), column_of(0, 1)
    mates = [(r, lax.rem(c + o, COLS)) for o in range(1, COLS)]
    z_mates = [(row_of(lax.rem(zh + o, 4), y, k), c) for o in range(1, 4)]
    y_mates = [(row_of(zh, lax.rem(y + o, 4), k), c) for o in range(1, 4)]
    other_core = (row_of(zh, y, 1 - k), c)
    target, part = r // 4, lax.rem(r, 4)
    offer_rows = [row_of(lax.rem(x + 2, 4), 2 * (1 - zl) + b, k) for b in range(2)]
    offer_senders = [(4 * c + 2 * g + k, lax.rem(zh + 2, 4) * 2 + 1 - y // 2) for g in range(2)]

    barrier = pltpu.get_barrier_semaphore()
    senders = mates + z_mates + y_mates + [other_core] + offer_senders
    for sender in senders:
        pl.semaphore_signal(barrier, inc=1, device_id=sender, device_id_type=MESH)

    loads = [
        pltpu.make_async_copy(src, dst, local_sem.at[i])
        for i, (src, dst) in enumerate(
            [(rows_ref, rows), (cols_ref, cols), (blocks_ref.at[0, 0], own.at[pl.ds(0, SLOTS)])]
        )
    ]
    for load in loads:
        load.start()
    for source in SOURCES:
        store[source][NONE] = jnp.zeros((BLK, BLK), jnp.bfloat16)
    for load in loads[:2]:
        load.wait()

    lane = lax.broadcasted_iota(jnp.int32, (8, 128), 1)
    found = jnp.full((8, 128), NONE, jnp.int32)
    live = counts_ref[0, 0]
    for s in range(SLOTS):
        position = jnp.where(s < live, rows[0, 0, s] * 2 + cols[0, 0, s], 127)
        found = jnp.where(lane == position, s, found)
    meta[0] = found
    load_own_table = pltpu.make_async_copy(meta.at[0], own_table, local_sem.at[3])
    load_own_table.start()
    load_own_table.wait()
    loads[2].wait()

    pl.semaphore_wait(barrier, len(senders))

    started = []

    def copy_to(src, dst, send_sem, recv_sem, device):
        return pltpu.make_async_remote_copy(
            src_ref=src, dst_ref=dst, send_sem=send_sem, recv_sem=recv_sem, device_id=device, device_id_type=MESH
        )

    def send(*what):
        copy = copy_to(*what)
        copy.start()
        started.append(copy)
        return copy

    left = {}

    def send_left(source, chunk, column, lands):
        first, size = CHUNKS[chunk]
        sem = len(left)
        left[(lands, chunk)] = send(
            store[source].at[pl.ds(first, size)], store[lands].at[pl.ds(first, size)],
            left_send.at[sem], left_recv.at[sem], (r, column),
        )

    def arrived(lands, *chunks):
        for chunk in chunks:
            left[(lands, chunk)].wait_recv()

    window_copies = [
        copy_to(window_ref, window, window_send.at[o], window_recv.at[0], mates[o]) for o in range(COLS - 1)
    ]
    home = target == c
    load_window = pltpu.make_async_copy(window_ref, window, local_sem.at[4])

    @pl.when(home)
    def _():
        load_window.start()
        for copy in window_copies:
            copy.start()

    send_left((0, 0), "ZA", to_pair, (0, 1))
    send_left((0, 0), "XA", to_right, (-1, 0))
    send_left((0, 0), "XB", to_left, (1, 0))
    send_left((0, 0), "XB", to_right, (-1, 0))
    send_left((0, 0), "XA", to_left, (1, 0))

    @pl.when(home)
    def _():
        load_window.wait()

    @pl.when(jnp.logical_not(home))
    def _():
        window_copies[0].wait_recv()

    for b in range(2):
        row = window[0, b] - part * RL
        mine = (row >= 0) & (row < RL)
        for j in range(2):
            place = jnp.where(mine, row, 0) * 2 + j
            picked[j, b] = own[jnp.where(mine, own_table[0, place], NONE)]
    pick_copy = send(picked.at[1 - k], given, pick_send.at[0], pick_recv.at[0], other_core)

    send_left((0, 0), "ZB", to_pair, (0, 1))
    send_left((0, 0), "ZA", to_right, (-1, 0))
    send_left((0, 0), "ZB", to_left, (1, 0))

    def add(one, other):
        return (one.astype(jnp.float32) + other.astype(jnp.float32)).astype(jnp.bfloat16)

    pick_copy.wait_recv()
    place_in_pair = lax.rem(y, 2)
    offer_copies = []
    for b in range(2):
        mixed[b] = add(picked[k, b], given[b])
        send(
            mixed.at[b], offered.at[place_in_pair], offer_send.at[b], offer_recv.at[place_in_pair],
            (offer_rows[b], target),
        )

    meta_copies = [
        send(meta.at[0], meta.at[o + 1], meta_send.at[o], meta_recv.at[o], mates[o]) for o in range(COLS - 1)
    ]
    send_left((0, 0), "ZB", to_right, (-1, 0))
    send_left((0, 0), "ZA", to_left, (1, 0))
    send_left((0, 0), "XA", to_pair, (0, 1))
    send_left((0, 0), "XB", to_pair, (0, 1))

    arrived((-1, 0), "XA")
    send_left((-1, 0), "XA", to_right, (2, 0))
    arrived((1, 0), "XB")
    send_left((1, 0), "XB", to_left, (2, 0))
    send_left((-1, 0), "XA", to_pair, (-1, 1))
    send_left((1, 0), "XB", to_pair, (1, 1))
    arrived((0, 1), "ZA")
    send_left((0, 1), "ZA", to_right, (-1, 1))
    send_left((0, 1), "ZA", to_left, (1, 1))

    for g in range(2):
        copy_to(
            mixed.at[g], offered.at[g], offer_send.at[g], offer_recv.at[g], (offer_rows[g], target)
        ).wait_recv()
    slab = y * 2 + k
    right[slab, zh] = add(offered[0], offered[1])

    def send_right(block, sem, device):
        return send(right.at[block], right.at[block], spread_send.at[sem], spread_recv.at[sem], device)

    z_copies = [send_right((slab, zh), o, z_mates[o]) for o in range(3)]
    y_copies = {}

    def spread_block(step):
        depth = lax.rem(zh + (4 - step), 4)
        for o in range(3):
            y_copies[(step, o)] = send_right((slab, depth), 3 + 3 * step + o, y_mates[o])

    spread_block(0)

    arrived((-1, 0), "XB")
    send_left((-1, 0), "XB", to_pair, (-1, 1))
    arrived((1, 0), "XA")
    send_left((1, 0), "XA", to_pair, (1, 1))
    arrived((0, 1), "ZB")
    send_left((0, 1), "ZB", to_left, (1, 1))
    send_left((0, 1), "ZB", to_right, (-1, 1))

    for step in (1, 3):
        z_copies[step - 1].wait_recv()
        spread_block(step)

    arrived((-1, 0), "ZA")
    send_left((-1, 0), "ZA", to_right, (2, 0))
    arrived((1, 0), "ZB")
    send_left((1, 0), "ZB", to_left, (2, 0))

    z_copies[1].wait_recv()
    spread_block(2)
    core_copies = [send_right(slab, 15, other_core)]

    arrived((2, 0), "XA", "XB")
    send_left((2, 0), "XA", to_pair, (2, 1))
    send_left((2, 0), "XB", to_pair, (2, 1))
    arrived((-1, 1), "ZA")
    send_left((-1, 1), "ZA", to_right, (2, 1))
    arrived((1, 1), "ZB")
    send_left((1, 1), "ZB", to_left, (2, 1))

    for copy in meta_copies:
        copy.wait_recv()
    load_table = pltpu.make_async_copy(meta, table, local_sem.at[5])
    load_table.start()

    for o in (0, 2, 1):
        for step in range(4):
            y_copies[(step, o)].wait_recv()
        core_copies.append(send_right(lax.rem(y + (3 - o), 4) * 2 + k, 16 + o, other_core))
    load_table.wait()
    for copy in core_copies:
        copy.wait_recv()

    def multiply(source, first):
        column = column_of(*source)
        entry = lax.rem(c - column + COLS, COLS)
        depth, base = lax.rem(column // 2 + 2, 4), 4 * (1 - lax.rem(column, 2))
        factor = jnp.concatenate(
            [
                jnp.concatenate([right[base + 2 * b + j, depth] for j in range(2)], axis=1)
                for b in range(2)
            ],
            axis=0,
        )
        strips = [
            jnp.concatenate([store[source][table[entry, 0, 2 * a + j]] for j in range(2)], axis=1) for a in range(RL)
        ]
        product = lax.dot_general(
            jnp.concatenate(strips, axis=0), factor, (((1,), (1,)), ((), ())), preferred_element_type=jnp.float32
        )
        for a in range(RL):
            for b in range(2):
                piece = product[a * BLK:(a + 1) * BLK, b * BLK:(b + 1) * BLK]
                if first:
                    out_ref[a, b] = piece
                else:
                    out_ref[a, b] += piece

    waits = {
        (0, 0): (),
        (0, 1): ("XA", "XB"),
        (-1, 0): ("ZB",),
        (1, 0): ("ZA",),
        (2, 0): ("ZA", "ZB"),
        (-1, 1): ("ZB", "XA", "XB"),
        (1, 1): ("ZA", "XA", "XB"),
        (2, 1): ("ZA", "ZB", "XA", "XB"),
    }
    for source in SOURCES:
        arrived(source, *waits[source])
        multiply(source, source == (0, 0))

    for copy in started:
        copy.wait_send()

    @pl.when(home)
    def _():
        for copy in window_copies:
            copy.wait_send()


def per_device(blocks, slot_rows, slot_cols, counts, col_window):
    operands = [
        pltpu.with_memory_space_constraint(value, pltpu.HBM)
        for value in (blocks, slot_rows, slot_cols, col_window)
    ]
    hbm = pl.BlockSpec(memory_space=pltpu.HBM)
    dma = pltpu.SemaphoreType.DMA
    return pl.pallas_call(
        kernel,
        out_shape=jax.ShapeDtypeStruct((RL, 2, BLK, BLK), jnp.float32),
        in_specs=[hbm] * 4 + [pl.BlockSpec(memory_space=pltpu.SMEM)],
        out_specs=pl.BlockSpec(memory_space=pltpu.VMEM),
        scratch_shapes=[
            *[pltpu.VMEM((SLOTS + 1, BLK, BLK), jnp.bfloat16) for _ in SOURCES],
            pltpu.SMEM(slot_rows.shape, jnp.int32),
            pltpu.SMEM(slot_cols.shape, jnp.int32),
            pltpu.SMEM(col_window.shape, jnp.int32),
            pltpu.VMEM((COLS, 8, 128), jnp.int32),
            pltpu.SMEM((COLS, 8, 128), jnp.int32),
            pltpu.SMEM((8, 128), jnp.int32),
            pltpu.VMEM((2, 2, BLK, BLK), jnp.bfloat16),
            pltpu.VMEM((2, BLK, BLK), jnp.bfloat16),
            pltpu.VMEM((2, BLK, BLK), jnp.bfloat16),
            pltpu.VMEM((2, BLK, BLK), jnp.bfloat16),
            pltpu.VMEM((8, 4, BLK, BLK), jnp.bfloat16),
            dma((28,)), dma((28,)), dma((7,)), dma((7,)), dma((7,)), dma((1,)), dma((1,)), dma((1,)),
            dma((2,)), dma((2,)), dma((19,)), dma((19,)), dma((6,)),
        ],
        compiler_params=pltpu.CompilerParams(
            collective_id=0, has_side_effects=True, vmem_limit_bytes=24 * 1024 * 1024
        ),
        cost_estimate=pl.CostEstimate(flops=2 * RL * BLK * 2048 * 256, bytes_accessed=8 * 1024 * 1024, transcendentals=0),
    )(*operands, counts)


def solution(mesh):
    placed = (
        P("row", "col", None, None, None),
        P("row", "col", None),
        P("row", "col", None),
        P("row", "col"),
        P("col", None),
    )
    return jax.shard_map(
        per_device, mesh=mesh, in_specs=placed, out_specs=P("row", "col", None, None), check_vma=False
    )
```

```python
import jax
import jax.numpy as jnp
from jax import lax
from jax.experimental import pallas as pl
from jax.experimental.pallas import tpu as pltpu
from jax.sharding import PartitionSpec as P

MESH = pl.DeviceIdType.MESH
BLK = 128
RL = 20
SLOTS = 16
NONE = SLOTS
COLS = 8

CHUNKS = {"ZA": (0, 5), "ZB": (5, 5), "XA": (10, 3), "XB": (13, 3)}
SOURCES = ((0, 0), (0, 1), (-1, 0), (1, 0), (2, 0), (-1, 1), (1, 1), (2, 1))


def kernel(
    blocks_ref, rows_ref, cols_ref, window_ref, counts_ref, out_ref,
    own, store_1, store_2, store_3, store_4, store_5, store_6, store_7,
    rows, cols, window, meta, table, own_table, picked, given, mixed, right,
    left_send, left_recv, meta_send, meta_recv, window_send, window_recv, pick_send, pick_recv,
    offer_send, offer_recv, spread_send, spread_recv, local_sem,
):
    r = lax.axis_index("row")
    c = lax.axis_index("col")
    zh, y, k = r // 8, lax.rem(r // 2, 4), lax.rem(r, 2)
    x, zl = c // 2, lax.rem(c, 2)
    store = dict(zip(SOURCES, (own, store_1, store_2, store_3, store_4, store_5, store_6, store_7)))

    def row_of(zh, y, k):
        return zh * 8 + y * 2 + k

    def column_of(dx, dz):
        return lax.rem(x + (dx + 4), 4) * 2 + (zl if dz == 0 else 1 - zl)

    to_right, to_left, to_pair = column_of(1, 0), column_of(-1, 0), column_of(0, 1)
    mates = [(r, lax.rem(c + o, COLS)) for o in range(1, COLS)]
    z_mates = [(row_of(lax.rem(zh + o, 4), y, k), c) for o in range(1, 4)]
    y_mates = [(row_of(zh, lax.rem(y + o, 4), k), c) for o in range(1, 4)]
    other_core = (row_of(zh, y, 1 - k), c)
    target, part = r // 4, lax.rem(r, 4)
    group = [(4 * target + lax.rem(part + o, 4), c) for o in range(1, 4)]
    offer_row = row_of(lax.rem(x + 2, 4), 2 * (1 - zl) + part // 2, k)
    offer_sender = (4 * c + lax.rem(y, 2) * 2 + k, lax.rem(zh + 2, 4) * 2 + 1 - y // 2)

    barrier = pltpu.get_barrier_semaphore()
    senders = mates + z_mates + y_mates + group + [offer_sender] + [other_core]
    for sender in senders:
        pl.semaphore_signal(barrier, inc=1, device_id=sender, device_id_type=MESH)

    loads = [
        pltpu.make_async_copy(src, dst, local_sem.at[i])
        for i, (src, dst) in enumerate(
            [(rows_ref, rows), (cols_ref, cols), (blocks_ref.at[0, 0], own.at[pl.ds(0, SLOTS)])]
        )
    ]
    for load in loads:
        load.start()
    for source in SOURCES:
        store[source][NONE] = jnp.zeros((BLK, BLK), jnp.bfloat16)
    for load in loads[:2]:
        load.wait()

    lane = lax.broadcasted_iota(jnp.int32, (8, 128), 1)
    found = jnp.full((8, 128), NONE, jnp.int32)
    live = counts_ref[0, 0]
    for s in range(SLOTS):
        position = jnp.where(s < live, rows[0, 0, s] * 2 + cols[0, 0, s], 127)
        found = jnp.where(lane == position, s, found)
    meta[0] = found
    load_own_table = pltpu.make_async_copy(meta.at[0], own_table, local_sem.at[3])
    load_own_table.start()
    load_own_table.wait()
    loads[2].wait()

    pl.semaphore_wait(barrier, len(senders))

    started = []

    def copy_to(src, dst, send_sem, recv_sem, device):
        return pltpu.make_async_remote_copy(
            src_ref=src, dst_ref=dst, send_sem=send_sem, recv_sem=recv_sem, device_id=device, device_id_type=MESH
        )

    def send(*what):
        copy = copy_to(*what)
        copy.start()
        started.append(copy)
        return copy

    left = {}

    def send_left(source, chunk, column, lands):
        first, size = CHUNKS[chunk]
        sem = len(left)
        left[(lands, chunk)] = send(
            store[source].at[pl.ds(first, size)], store[lands].at[pl.ds(first, size)],
            left_send.at[sem], left_recv.at[sem], (r, column),
        )

    def arrived(lands, *chunks):
        for chunk in chunks:
            left[(lands, chunk)].wait_recv()

    window_copies = [
        copy_to(window_ref, window, window_send.at[o], window_recv.at[0], mates[o]) for o in range(COLS - 1)
    ]
    home = target == c
    load_window = pltpu.make_async_copy(window_ref, window, local_sem.at[4])

    @pl.when(home)
    def _():
        load_window.start()
        for copy in window_copies:
            copy.start()

    send_left((0, 0), "ZA", to_pair, (0, 1))
    send_left((0, 0), "XA", to_right, (-1, 0))
    send_left((0, 0), "XB", to_left, (1, 0))
    send_left((0, 0), "XB", to_right, (-1, 0))
    send_left((0, 0), "XA", to_left, (1, 0))

    @pl.when(home)
    def _():
        load_window.wait()

    @pl.when(jnp.logical_not(home))
    def _():
        window_copies[0].wait_recv()

    for b in range(2):
        row = window[0, b] - part * RL
        mine = (row >= 0) & (row < RL)
        for j in range(2):
            place = jnp.where(mine, row, 0) * 2 + j
            picked[2 * b + j] = own[jnp.where(mine, own_table[0, place], NONE)]
    pick_copies = [
        send(picked.at[lax.rem(part + o, 4)], given.at[o - 1], pick_send.at[o - 1], pick_recv.at[o - 1], group[o - 1])
        for o in range(1, 4)
    ]
    for copy in pick_copies:
        copy.wait_recv()
    total = picked[part].astype(jnp.float32)
    for o in range(3):
        total = total + given[o].astype(jnp.float32)
    mixed[...] = total.astype(jnp.bfloat16)
    slab = y * 2 + k
    offer_copy = send(mixed, right.at[2 * (2 * (1 - zl) + part // 2) + k, lax.rem(x + 2, 4)], offer_send.at[0], offer_recv.at[0], (offer_row, target))
    meta_copies = [
        send(meta.at[0], meta.at[o + 1], meta_send.at[o], meta_recv.at[o], mates[o]) for o in range(COLS - 1)
    ]

    send_left((0, 0), "ZB", to_pair, (0, 1))
    send_left((0, 0), "ZA", to_right, (-1, 0))
    send_left((0, 0), "ZB", to_left, (1, 0))
    send_left((0, 0), "ZB", to_right, (-1, 0))
    send_left((0, 0), "ZA", to_left, (1, 0))
    send_left((0, 0), "XA", to_pair, (0, 1))
    send_left((0, 0), "XB", to_pair, (0, 1))

    arrived((-1, 0), "XA")
    send_left((-1, 0), "XA", to_right, (2, 0))
    arrived((1, 0), "XB")
    send_left((1, 0), "XB", to_left, (2, 0))
    arrived((0, 1), "ZA")
    send_left((0, 1), "ZA", to_right, (-1, 1))
    send_left((0, 1), "ZA", to_left, (1, 1))
    offer_copy.wait_recv()

    def send_right(block, sem, device):
        return send(right.at[block], right.at[block], spread_send.at[sem], spread_recv.at[sem], device)

    z_copies = [send_right((slab, zh), o, z_mates[o]) for o in range(3)]
    y_copies = {}

    def spread_block(step):
        depth = lax.rem(zh + (4 - step), 4)
        for o in range(3):
            y_copies[(step, o)] = send_right((slab, depth), 3 + 3 * step + o, y_mates[o])

    spread_block(0)

    send_left((-1, 0), "XA", to_pair, (-1, 1))
    send_left((1, 0), "XB", to_pair, (1, 1))
    arrived((-1, 0), "XB")
    send_left((-1, 0), "XB", to_pair, (-1, 1))
    arrived((1, 0), "XA")
    send_left((1, 0), "XA", to_pair, (1, 1))
    arrived((0, 1), "ZB")
    send_left((0, 1), "ZB", to_left, (1, 1))
    send_left((0, 1), "ZB", to_right, (-1, 1))
    arrived((-1, 0), "ZA")
    send_left((-1, 0), "ZA", to_right, (2, 0))
    arrived((1, 0), "ZB")
    send_left((1, 0), "ZB", to_left, (2, 0))

    for step in (1, 3):
        z_copies[step - 1].wait_recv()
        spread_block(step)
    z_copies[1].wait_recv()
    spread_block(2)
    core_copies = [send_right(slab, 15, other_core)]

    arrived((2, 0), "XA", "XB")
    send_left((2, 0), "XA", to_pair, (2, 1))
    send_left((2, 0), "XB", to_pair, (2, 1))
    arrived((-1, 1), "ZA")
    send_left((-1, 1), "ZA", to_right, (2, 1))
    arrived((1, 1), "ZB")
    send_left((1, 1), "ZB", to_left, (2, 1))

    for copy in meta_copies:
        copy.wait_recv()
    load_table = pltpu.make_async_copy(meta, table, local_sem.at[5])
    load_table.start()

    for o in (0, 2, 1):
        for step in range(4):
            y_copies[(step, o)].wait_recv()
        core_copies.append(send_right(lax.rem(y + (3 - o), 4) * 2 + k, 16 + o, other_core))
    load_table.wait()
    for copy in core_copies:
        copy.wait_recv()

    def multiply(source, first):
        column = column_of(*source)
        entry = lax.rem(c - column + COLS, COLS)
        depth, base = lax.rem(column // 2 + 2, 4), 4 * (1 - lax.rem(column, 2))
        factor = jnp.concatenate(
            [
                jnp.concatenate([right[base + 2 * b + j, depth] for j in range(2)], axis=1)
                for b in range(2)
            ],
            axis=0,
        )
        strips = [
            jnp.concatenate([store[source][table[entry, 0, 2 * a + j]] for j in range(2)], axis=1) for a in range(RL)
        ]
        product = lax.dot_general(
            jnp.concatenate(strips, axis=0), factor, (((1,), (1,)), ((), ())), preferred_element_type=jnp.float32
        )
        for a in range(RL):
            for b in range(2):
                piece = product[a * BLK:(a + 1) * BLK, b * BLK:(b + 1) * BLK]
                if first:
                    out_ref[a, b] = piece
                else:
                    out_ref[a, b] += piece

    waits = {
        (0, 0): (),
        (0, 1): ("XA", "XB"),
        (-1, 0): ("ZB",),
        (1, 0): ("ZA",),
        (2, 0): ("ZA", "ZB"),
        (-1, 1): ("ZB", "XA", "XB"),
        (1, 1): ("ZA", "XA", "XB"),
        (2, 1): ("ZA", "ZB", "XA", "XB"),
    }
    for source in SOURCES:
        arrived(source, *waits[source])
        multiply(source, source == (0, 0))

    for copy in started:
        copy.wait_send()

    @pl.when(home)
    def _():
        for copy in window_copies:
            copy.wait_send()


def per_device(blocks, slot_rows, slot_cols, counts, col_window):
    operands = [
        pltpu.with_memory_space_constraint(value, pltpu.HBM)
        for value in (blocks, slot_rows, slot_cols, col_window)
    ]
    hbm = pl.BlockSpec(memory_space=pltpu.HBM)
    dma = pltpu.SemaphoreType.DMA
    return pl.pallas_call(
        kernel,
        out_shape=jax.ShapeDtypeStruct((RL, 2, BLK, BLK), jnp.float32),
        in_specs=[hbm] * 4 + [pl.BlockSpec(memory_space=pltpu.SMEM)],
        out_specs=pl.BlockSpec(memory_space=pltpu.VMEM),
        scratch_shapes=[
            *[pltpu.VMEM((SLOTS + 1, BLK, BLK), jnp.bfloat16) for _ in SOURCES],
            pltpu.SMEM(slot_rows.shape, jnp.int32),
            pltpu.SMEM(slot_cols.shape, jnp.int32),
            pltpu.SMEM(col_window.shape, jnp.int32),
            pltpu.VMEM((COLS, 8, 128), jnp.int32),
            pltpu.SMEM((COLS, 8, 128), jnp.int32),
            pltpu.SMEM((8, 128), jnp.int32),
            pltpu.VMEM((4, BLK, BLK), jnp.bfloat16),
            pltpu.VMEM((3, BLK, BLK), jnp.bfloat16),
            pltpu.VMEM((BLK, BLK), jnp.bfloat16),
            pltpu.VMEM((8, 4, BLK, BLK), jnp.bfloat16),
            dma((28,)), dma((28,)), dma((7,)), dma((7,)), dma((7,)), dma((1,)), dma((3,)), dma((3,)),
            dma((1,)), dma((1,)), dma((19,)), dma((19,)), dma((6,)),
        ],
        compiler_params=pltpu.CompilerParams(
            collective_id=0, has_side_effects=True, vmem_limit_bytes=24 * 1024 * 1024
        ),
        cost_estimate=pl.CostEstimate(flops=2 * RL * BLK * 2048 * 256, bytes_accessed=8 * 1024 * 1024, transcendentals=0),
    )(*operands, counts)


def solution(mesh):
    placed = (
        P("row", "col", None, None, None),
        P("row", "col", None),
        P("row", "col", None),
        P("row", "col"),
        P("col", None),
    )
    return jax.shard_map(
        per_device, mesh=mesh, in_specs=placed, out_specs=P("row", "col", None, None), check_vma=False
    )
```

```python
import jax
import jax.numpy as jnp
from jax import lax
from jax.experimental import pallas as pl
from jax.experimental.pallas import tpu as pltpu
from jax.sharding import PartitionSpec as P

MESH = pl.DeviceIdType.MESH
BLK = 128
RL = 20
SLOTS = 16
NONE = SLOTS
COLS = 8

CHUNKS = {"ZA": (0, 5), "ZB": (5, 5), "XA": (10, 3), "XB": (13, 3)}
SOURCES = ((0, 0), (0, 1), (-1, 0), (1, 0), (2, 0), (-1, 1), (1, 1), (2, 1))


def kernel(
    blocks_ref, rows_ref, cols_ref, window_ref, counts_ref, out_ref,
    own, store_1, store_2, store_3, store_4, store_5, store_6, store_7,
    rows, cols, window, meta, table, own_table, picked, given, mixed, right,
    left_send, left_recv, meta_send, meta_recv, window_send, window_recv, pick_send, pick_recv,
    offer_send, offer_recv, spread_send, spread_recv, local_sem,
):
    r = lax.axis_index("row")
    c = lax.axis_index("col")
    zh, y, k = r // 8, lax.rem(r // 2, 4), lax.rem(r, 2)
    x, zl = c // 2, lax.rem(c, 2)
    store = dict(zip(SOURCES, (own, store_1, store_2, store_3, store_4, store_5, store_6, store_7)))

    def row_of(zh, y, k):
        return zh * 8 + y * 2 + k

    def column_of(dx, dz):
        return lax.rem(x + (dx + 4), 4) * 2 + (zl if dz == 0 else 1 - zl)

    def held_at(column, partner, owner):
        turned = jnp.where(lax.rem(column + owner, 2) == 0, 1 - partner, partner)
        return 2 * (1 - lax.rem(column, 2)) + turned

    to_right, to_left, to_pair = column_of(1, 0), column_of(-1, 0), column_of(0, 1)
    mates = [(r, lax.rem(c + o, COLS)) for o in range(1, COLS)]
    z_mates = [(row_of(lax.rem(zh + o, 4), y, k), c) for o in range(1, 4)]
    y_mates = [(row_of(zh, lax.rem(y + o, 4), k), c) for o in range(1, 4)]
    other_core = (row_of(zh, y, 1 - k), c)
    target, part = r // 4, lax.rem(r, 4)
    group = [(4 * target + lax.rem(part + o, 4), c) for o in range(1, 4)]
    offer_y = held_at(c, part // 2, target)
    offer_row = row_of(lax.rem(x + 2, 4), offer_y, k)
    sender_column = lax.rem(zh + 2, 4) * 2 + 1 - y // 2
    near = jnp.where(lax.rem(sender_column + c, 2) == 0, 1 - lax.rem(y, 2), lax.rem(y, 2))
    offer_sender = (4 * c + 2 * near + k, sender_column)

    barrier = pltpu.get_barrier_semaphore()
    senders = mates + z_mates + y_mates + group + [offer_sender] + [other_core]
    for sender in senders:
        pl.semaphore_signal(barrier, inc=1, device_id=sender, device_id_type=MESH)

    loads = [
        pltpu.make_async_copy(src, dst, local_sem.at[i])
        for i, (src, dst) in enumerate(
            [(rows_ref, rows), (cols_ref, cols), (blocks_ref.at[0, 0], own.at[pl.ds(0, SLOTS)])]
        )
    ]
    for load in loads:
        load.start()
    for source in SOURCES:
        store[source][NONE] = jnp.zeros((BLK, BLK), jnp.bfloat16)
    for load in loads[:2]:
        load.wait()

    lane = lax.broadcasted_iota(jnp.int32, (8, 128), 1)
    found = jnp.full((8, 128), NONE, jnp.int32)
    live = counts_ref[0, 0]
    for s in range(SLOTS):
        position = jnp.where(s < live, rows[0, 0, s] * 2 + cols[0, 0, s], 127)
        found = jnp.where(lane == position, s, found)
    meta[0] = found
    load_own_table = pltpu.make_async_copy(meta.at[0], own_table, local_sem.at[3])
    load_own_table.start()
    load_own_table.wait()
    loads[2].wait()

    pl.semaphore_wait(barrier, len(senders))

    started = []

    def copy_to(src, dst, send_sem, recv_sem, device):
        return pltpu.make_async_remote_copy(
            src_ref=src, dst_ref=dst, send_sem=send_sem, recv_sem=recv_sem, device_id=device, device_id_type=MESH
        )

    def send(*what):
        copy = copy_to(*what)
        copy.start()
        started.append(copy)
        return copy

    left, seen = {}, set()

    def send_left(source, chunk, column, lands):
        first, size = CHUNKS[chunk]
        sem = len(left)
        left[(lands, chunk)] = send(
            store[source].at[pl.ds(first, size)], store[lands].at[pl.ds(first, size)],
            left_send.at[sem], left_recv.at[sem], (r, column),
        )

    def arrived(lands, *chunks):
        for chunk in chunks:
            if (lands, chunk) not in seen:
                seen.add((lands, chunk))
                left[(lands, chunk)].wait_recv()

    window_copies = [
        copy_to(window_ref, window, window_send.at[o], window_recv.at[0], mates[o]) for o in range(COLS - 1)
    ]
    home = target == c
    load_window = pltpu.make_async_copy(window_ref, window, local_sem.at[4])

    @pl.when(home)
    def _():
        load_window.start()
        for copy in window_copies:
            copy.start()

    send_left((0, 0), "ZA", to_pair, (0, 1))

    send_left((0, 0), "XA", to_right, (-1, 0))
    send_left((0, 0), "XB", to_left, (1, 0))

    send_left((0, 0), "XB", to_right, (-1, 0))
    send_left((0, 0), "XA", to_left, (1, 0))

    send_left((0, 0), "ZB", to_pair, (0, 1))

    send_left((0, 0), "ZA", to_right, (-1, 0))
    send_left((0, 0), "ZB", to_left, (1, 0))

    @pl.when(home)
    def _():
        load_window.wait()

    @pl.when(jnp.logical_not(home))
    def _():
        window_copies[0].wait_recv()

    for b in range(2):
        row = window[0, b] - part * RL
        mine = (row >= 0) & (row < RL)
        for j in range(2):
            place = jnp.where(mine, row, 0) * 2 + j
            picked[2 * b + j] = own[jnp.where(mine, own_table[0, place], NONE)]
    pick_copies = [
        send(picked.at[lax.rem(part + o, 4)], given.at[o - 1], pick_send.at[o - 1], pick_recv.at[o - 1], group[o - 1])
        for o in range(1, 4)
    ]

    for copy in pick_copies:
        copy.wait_recv()
    total = picked[part].astype(jnp.float32)
    for o in range(3):
        total = total + given[o].astype(jnp.float32)
    mixed[...] = total.astype(jnp.bfloat16)
    slab = y * 2 + k
    offer_copy = send(mixed, right.at[2 * offer_y + k, lax.rem(x + 2, 4)], offer_send.at[0], offer_recv.at[0], (offer_row, target))

    send_left((0, 0), "ZB", to_right, (-1, 0))
    send_left((0, 0), "ZA", to_left, (1, 0))

    send_left((0, 0), "XA", to_pair, (0, 1))

    send_left((0, 0), "XB", to_pair, (0, 1))

    arrived((-1, 0), "XA")
    send_left((-1, 0), "XA", to_right, (2, 0))
    arrived((1, 0), "XB")
    send_left((1, 0), "XB", to_left, (2, 0))

    arrived((0, 1), "ZA")
    send_left((0, 1), "ZA", to_right, (-1, 1))
    arrived((0, 1), "ZB")
    send_left((0, 1), "ZB", to_left, (1, 1))

    offer_copy.wait_recv()

    def send_right(block, sem, device):
        return send(right.at[block], right.at[block], spread_send.at[sem], spread_recv.at[sem], device)

    z_copies = [send_right((slab, zh), o, z_mates[o]) for o in range(3)]
    y_copies = {}

    def spread_block(step):
        depth = lax.rem(zh + (4 - step), 4)
        for o in range(3):
            y_copies[(step, o)] = send_right((slab, depth), 3 + 3 * step + o, y_mates[o])

    spread_block(0)

    arrived((-1, 0), "XA")
    send_left((-1, 0), "XA", to_pair, (-1, 1))
    arrived((1, 0), "XB")
    send_left((1, 0), "XB", to_pair, (1, 1))

    meta_copies = [
        send(meta.at[0], meta.at[o + 1], meta_send.at[o], meta_recv.at[o], mates[o]) for o in range(COLS - 1)
    ]

    arrived((-1, 0), "XB")
    send_left((-1, 0), "XB", to_pair, (-1, 1))
    arrived((1, 0), "XA")
    send_left((1, 0), "XA", to_pair, (1, 1))

    arrived((-1, 0), "ZA")
    send_left((-1, 0), "ZA", to_right, (2, 0))
    arrived((1, 0), "ZB")
    send_left((1, 0), "ZB", to_left, (2, 0))

    send_left((0, 1), "ZB", to_right, (-1, 1))
    send_left((0, 1), "ZA", to_left, (1, 1))

    for step in (1, 3):
        z_copies[step - 1].wait_recv()
        spread_block(step)

    z_copies[1].wait_recv()
    spread_block(2)
    core_copies = [send_right(slab, 15, other_core)]

    arrived((2, 0), "XA", "XB")
    send_left((2, 0), "XA", to_pair, (2, 1))
    send_left((2, 0), "XB", to_pair, (2, 1))

    arrived((-1, 1), "ZA")
    send_left((-1, 1), "ZA", to_right, (2, 1))
    arrived((1, 1), "ZB")
    send_left((1, 1), "ZB", to_left, (2, 1))

    for copy in meta_copies:
        copy.wait_recv()
    load_table = pltpu.make_async_copy(meta, table, local_sem.at[5])
    load_table.start()

    for o in (0, 2, 1):
        for step in range(4):
            y_copies[(step, o)].wait_recv()
        core_copies.append(send_right(lax.rem(y + (3 - o), 4) * 2 + k, 16 + o, other_core))

    load_table.wait()
    for copy in core_copies:
        copy.wait_recv()

    def multiply(source, first):
        column = column_of(*source)
        entry = lax.rem(c - column + COLS, COLS)
        depth = lax.rem(column // 2 + 2, 4)
        factor = jnp.concatenate(
            [
                jnp.concatenate([right[2 * held_at(column, b, c) + j, depth] for j in range(2)], axis=1)
                for b in range(2)
            ],
            axis=0,
        )
        strips = [
            jnp.concatenate([store[source][table[entry, 0, 2 * a + j]] for j in range(2)], axis=1) for a in range(RL)
        ]
        product = lax.dot_general(
            jnp.concatenate(strips, axis=0), factor, (((1,), (1,)), ((), ())), preferred_element_type=jnp.float32
        )
        for a in range(RL):
            for b in range(2):
                piece = product[a * BLK:(a + 1) * BLK, b * BLK:(b + 1) * BLK]
                if first:
                    out_ref[a, b] = piece
                else:
                    out_ref[a, b] += piece

    waits = {
        (0, 0): (),
        (0, 1): ("XA", "XB"),
        (-1, 0): ("ZB",),
        (1, 0): ("ZA",),
        (2, 0): ("ZA", "ZB"),
        (-1, 1): ("ZB", "XA", "XB"),
        (1, 1): ("ZA", "XA", "XB"),
        (2, 1): ("ZA", "ZB", "XA", "XB"),
    }
    for source in SOURCES:
        arrived(source, *waits[source])
        multiply(source, source == (0, 0))

    for copy in started:
        copy.wait_send()

    @pl.when(home)
    def _():
        for copy in window_copies:
            copy.wait_send()


def per_device(blocks, slot_rows, slot_cols, counts, col_window):
    operands = [
        pltpu.with_memory_space_constraint(value, pltpu.HBM)
        for value in (blocks, slot_rows, slot_cols, col_window)
    ]
    hbm = pl.BlockSpec(memory_space=pltpu.HBM)
    dma = pltpu.SemaphoreType.DMA
    return pl.pallas_call(
        kernel,
        out_shape=jax.ShapeDtypeStruct((RL, 2, BLK, BLK), jnp.float32),
        in_specs=[hbm] * 4 + [pl.BlockSpec(memory_space=pltpu.SMEM)],
        out_specs=pl.BlockSpec(memory_space=pltpu.VMEM),
        scratch_shapes=[
            *[pltpu.VMEM((SLOTS + 1, BLK, BLK), jnp.bfloat16) for _ in SOURCES],
            pltpu.SMEM(slot_rows.shape, jnp.int32),
            pltpu.SMEM(slot_cols.shape, jnp.int32),
            pltpu.SMEM(col_window.shape, jnp.int32),
            pltpu.VMEM((COLS, 8, 128), jnp.int32),
            pltpu.SMEM((COLS, 8, 128), jnp.int32),
            pltpu.SMEM((8, 128), jnp.int32),
            pltpu.VMEM((4, BLK, BLK), jnp.bfloat16),
            pltpu.VMEM((3, BLK, BLK), jnp.bfloat16),
            pltpu.VMEM((BLK, BLK), jnp.bfloat16),
            pltpu.VMEM((8, 4, BLK, BLK), jnp.bfloat16),
            dma((28,)), dma((28,)), dma((7,)), dma((7,)), dma((7,)), dma((1,)), dma((3,)), dma((3,)),
            dma((1,)), dma((1,)), dma((19,)), dma((19,)), dma((6,)),
        ],
        compiler_params=pltpu.CompilerParams(
            collective_id=0, has_side_effects=True, vmem_limit_bytes=24 * 1024 * 1024
        ),
        cost_estimate=pl.CostEstimate(flops=2 * RL * BLK * 2048 * 256, bytes_accessed=8 * 1024 * 1024, transcendentals=0),
    )(*operands, counts)


def solution(mesh):
    placed = (
        P("row", "col", None, None, None),
        P("row", "col", None),
        P("row", "col", None),
        P("row", "col"),
        P("col", None),
    )
    return jax.shard_map(
        per_device, mesh=mesh, in_specs=placed, out_specs=P("row", "col", None, None), check_vma=False
    )
```

```python
import jax
import jax.numpy as jnp
from jax import lax
from jax.experimental import pallas as pl
from jax.experimental.pallas import tpu as pltpu
from jax.sharding import PartitionSpec as P

MESH = pl.DeviceIdType.MESH
BLK = 128
RL = 20
SLOTS = 16
NONE = SLOTS
COLS = 8

CHUNKS = {"ZA": (0, 5), "ZB": (5, 5), "XA": (10, 3), "XB": (13, 3)}
SOURCES = ((0, 0), (0, 1), (-1, 0), (1, 0), (2, 0), (-1, 1), (1, 1), (2, 1))


def kernel(
    blocks_ref, rows_ref, cols_ref, window_ref, counts_ref, out_ref,
    own, store_1, store_2, store_3, store_4, store_5, store_6, store_7,
    rows, cols, window, meta, table, own_table, picked, given, mixed, right,
    left_send, left_recv, meta_send, meta_recv, window_send, window_recv, pick_send, pick_recv,
    offer_send, offer_recv, spread_send, spread_recv, local_sem,
):
    r = lax.axis_index("row")
    c = lax.axis_index("col")
    zh, y, k = r // 8, lax.rem(r // 2, 4), lax.rem(r, 2)
    x, zl = c // 2, lax.rem(c, 2)
    store = dict(zip(SOURCES, (own, store_1, store_2, store_3, store_4, store_5, store_6, store_7)))

    def row_of(zh, y, k):
        return zh * 8 + y * 2 + k

    def column_of(dx, dz):
        return lax.rem(x + (dx + 4), 4) * 2 + (zl if dz == 0 else 1 - zl)

    def held_at(column, partner, owner):
        turned = jnp.where(lax.rem(column + owner, 2) == 0, 1 - partner, partner)
        return 2 * (1 - lax.rem(column, 2)) + turned

    to_right, to_left, to_pair = column_of(1, 0), column_of(-1, 0), column_of(0, 1)
    mates = [(r, lax.rem(c + o, COLS)) for o in range(1, COLS)]
    z_mates = [(row_of(lax.rem(zh + o, 4), y, k), c) for o in range(1, 4)]
    y_mates = [(row_of(zh, lax.rem(y + o, 4), k), c) for o in range(1, 4)]
    other_core = (row_of(zh, y, 1 - k), c)
    target, part = r // 4, lax.rem(r, 4)
    group = [(4 * target + lax.rem(part + o, 4), c) for o in range(1, 4)]
    offer_y = held_at(c, part // 2, target)
    offer_row = row_of(lax.rem(x + 2, 4), offer_y, k)
    sender_column = lax.rem(zh + 2, 4) * 2 + 1 - y // 2
    near = jnp.where(lax.rem(sender_column + c, 2) == 0, 1 - lax.rem(y, 2), lax.rem(y, 2))
    offer_sender = (4 * c + 2 * near + k, sender_column)

    loads = [
        pltpu.make_async_copy(src, dst, local_sem.at[i])
        for i, (src, dst) in enumerate(
            [(rows_ref, rows), (cols_ref, cols), (blocks_ref.at[0, 0], own.at[pl.ds(0, SLOTS)])]
        )
    ]
    for load in loads:
        load.start()

    barrier = pltpu.get_barrier_semaphore()
    senders = mates + z_mates + y_mates + group + [offer_sender] + [other_core]
    for sender in senders:
        pl.semaphore_signal(barrier, inc=1, device_id=sender, device_id_type=MESH)

    pl.semaphore_wait(barrier, len(senders))

    started = []

    def copy_to(src, dst, send_sem, recv_sem, device):
        return pltpu.make_async_remote_copy(
            src_ref=src, dst_ref=dst, send_sem=send_sem, recv_sem=recv_sem, device_id=device, device_id_type=MESH
        )

    def send(*what):
        copy = copy_to(*what)
        copy.start()
        started.append(copy)
        return copy

    left, seen = {}, set()

    def send_left(source, chunk, column, lands):
        first, size = CHUNKS[chunk]
        sem = len(left)
        left[(lands, chunk)] = send(
            store[source].at[pl.ds(first, size)], store[lands].at[pl.ds(first, size)],
            left_send.at[sem], left_recv.at[sem], (r, column),
        )

    def arrived(lands, *chunks):
        for chunk in chunks:
            if (lands, chunk) not in seen:
                seen.add((lands, chunk))
                left[(lands, chunk)].wait_recv()

    window_copies = [
        copy_to(window_ref, window, window_send.at[o], window_recv.at[0], mates[o]) for o in range(COLS - 1)
    ]
    home = target == c
    load_window = pltpu.make_async_copy(window_ref, window, local_sem.at[4])

    @pl.when(home)
    def _():
        load_window.start()
        for copy in window_copies:
            copy.start()

    loads[2].wait()
    send_left((0, 0), "ZA", to_pair, (0, 1))

    send_left((0, 0), "XA", to_right, (-1, 0))
    send_left((0, 0), "XB", to_left, (1, 0))

    send_left((0, 0), "XB", to_right, (-1, 0))
    send_left((0, 0), "XA", to_left, (1, 0))

    send_left((0, 0), "ZB", to_pair, (0, 1))

    send_left((0, 0), "ZA", to_right, (-1, 0))
    send_left((0, 0), "ZB", to_left, (1, 0))

    for source in SOURCES:
        store[source][NONE] = jnp.zeros((BLK, BLK), jnp.bfloat16)
    for load in loads[:2]:
        load.wait()

    lane = lax.broadcasted_iota(jnp.int32, (8, 128), 1)
    found = jnp.full((8, 128), NONE, jnp.int32)
    live = counts_ref[0, 0]
    for s in range(SLOTS):
        position = jnp.where(s < live, rows[0, 0, s] * 2 + cols[0, 0, s], 127)
        found = jnp.where(lane == position, s, found)
    meta[0] = found
    load_own_table = pltpu.make_async_copy(meta.at[0], own_table, local_sem.at[3])
    load_own_table.start()
    load_own_table.wait()

    @pl.when(home)
    def _():
        load_window.wait()

    @pl.when(jnp.logical_not(home))
    def _():
        window_copies[0].wait_recv()

    for b in range(2):
        row = window[0, b] - part * RL
        mine = (row >= 0) & (row < RL)
        for j in range(2):
            place = jnp.where(mine, row, 0) * 2 + j
            picked[2 * b + j] = own[jnp.where(mine, own_table[0, place], NONE)]
    pick_copies = [
        send(picked.at[lax.rem(part + o, 4)], given.at[o - 1], pick_send.at[o - 1], pick_recv.at[o - 1], group[o - 1])
        for o in range(1, 4)
    ]

    for copy in pick_copies:
        copy.wait_recv()
    total = picked[part].astype(jnp.float32)
    for o in range(3):
        total = total + given[o].astype(jnp.float32)
    mixed[...] = total.astype(jnp.bfloat16)
    slab = y * 2 + k
    offer_copy = send(mixed, right.at[2 * offer_y + k, lax.rem(x + 2, 4)], offer_send.at[0], offer_recv.at[0], (offer_row, target))

    send_left((0, 0), "ZB", to_right, (-1, 0))
    send_left((0, 0), "ZA", to_left, (1, 0))

    send_left((0, 0), "XA", to_pair, (0, 1))

    send_left((0, 0), "XB", to_pair, (0, 1))

    arrived((-1, 0), "XA")
    send_left((-1, 0), "XA", to_right, (2, 0))
    arrived((1, 0), "XB")
    send_left((1, 0), "XB", to_left, (2, 0))

    arrived((0, 1), "ZA")
    send_left((0, 1), "ZA", to_right, (-1, 1))
    arrived((0, 1), "ZB")
    send_left((0, 1), "ZB", to_left, (1, 1))

    offer_copy.wait_recv()

    def send_right(block, sem, device):
        return send(right.at[block], right.at[block], spread_send.at[sem], spread_recv.at[sem], device)

    z_copies = [send_right((slab, zh), o, z_mates[o]) for o in range(3)]
    y_copies = {}

    def spread_block(step):
        depth = lax.rem(zh + (4 - step), 4)
        for o in range(3):
            y_copies[(step, o)] = send_right((slab, depth), 3 + 3 * step + o, y_mates[o])

    spread_block(0)

    arrived((-1, 0), "XA")
    send_left((-1, 0), "XA", to_pair, (-1, 1))
    arrived((1, 0), "XB")
    send_left((1, 0), "XB", to_pair, (1, 1))

    meta_copies = [
        send(meta.at[0], meta.at[o + 1], meta_send.at[o], meta_recv.at[o], mates[o]) for o in range(COLS - 1)
    ]

    arrived((-1, 0), "XB")
    send_left((-1, 0), "XB", to_pair, (-1, 1))
    arrived((1, 0), "XA")
    send_left((1, 0), "XA", to_pair, (1, 1))

    arrived((-1, 0), "ZA")
    send_left((-1, 0), "ZA", to_right, (2, 0))
    arrived((1, 0), "ZB")
    send_left((1, 0), "ZB", to_left, (2, 0))

    send_left((0, 1), "ZB", to_right, (-1, 1))
    send_left((0, 1), "ZA", to_left, (1, 1))

    for step in (1, 3):
        z_copies[step - 1].wait_recv()
        spread_block(step)

    z_copies[1].wait_recv()
    spread_block(2)
    core_copies = [send_right(slab, 15, other_core)]

    arrived((2, 0), "XA", "XB")
    send_left((2, 0), "XA", to_pair, (2, 1))
    send_left((2, 0), "XB", to_pair, (2, 1))

    arrived((-1, 1), "ZA")
    send_left((-1, 1), "ZA", to_right, (2, 1))
    arrived((1, 1), "ZB")
    send_left((1, 1), "ZB", to_left, (2, 1))

    for copy in meta_copies:
        copy.wait_recv()
    load_table = pltpu.make_async_copy(meta, table, local_sem.at[5])
    load_table.start()

    for o in (0, 2, 1):
        for step in range(4):
            y_copies[(step, o)].wait_recv()
        core_copies.append(send_right(lax.rem(y + (3 - o), 4) * 2 + k, 16 + o, other_core))

    load_table.wait()
    for copy in core_copies:
        copy.wait_recv()

    def multiply(source, first):
        column = column_of(*source)
        entry = lax.rem(c - column + COLS, COLS)
        depth = lax.rem(column // 2 + 2, 4)
        factor = jnp.concatenate(
            [
                jnp.concatenate([right[2 * held_at(column, b, c) + j, depth] for j in range(2)], axis=1)
                for b in range(2)
            ],
            axis=0,
        )
        strips = [
            jnp.concatenate([store[source][table[entry, 0, 2 * a + j]] for j in range(2)], axis=1) for a in range(RL)
        ]
        product = lax.dot_general(
            jnp.concatenate(strips, axis=0), factor, (((1,), (1,)), ((), ())), preferred_element_type=jnp.float32
        )
        for a in range(RL):
            for b in range(2):
                piece = product[a * BLK:(a + 1) * BLK, b * BLK:(b + 1) * BLK]
                if first:
                    out_ref[a, b] = piece
                else:
                    out_ref[a, b] += piece

    waits = {
        (0, 0): (),
        (0, 1): ("XA", "XB"),
        (-1, 0): ("ZB",),
        (1, 0): ("ZA",),
        (2, 0): ("ZA", "ZB"),
        (-1, 1): ("ZB", "XA", "XB"),
        (1, 1): ("ZA", "XA", "XB"),
        (2, 1): ("ZA", "ZB", "XA", "XB"),
    }
    for group in (SOURCES[:5], SOURCES[5:]):
        for source in group:
            arrived(source, *waits[source])
        for source in group:
            multiply(source, source == (0, 0))

    for copy in started:
        copy.wait_send()

    @pl.when(home)
    def _():
        for copy in window_copies:
            copy.wait_send()


def per_device(blocks, slot_rows, slot_cols, counts, col_window):
    operands = [
        pltpu.with_memory_space_constraint(value, pltpu.HBM)
        for value in (blocks, slot_rows, slot_cols, col_window)
    ]
    hbm = pl.BlockSpec(memory_space=pltpu.HBM)
    dma = pltpu.SemaphoreType.DMA
    return pl.pallas_call(
        kernel,
        out_shape=jax.ShapeDtypeStruct((RL, 2, BLK, BLK), jnp.float32),
        in_specs=[hbm] * 4 + [pl.BlockSpec(memory_space=pltpu.SMEM)],
        out_specs=pl.BlockSpec(memory_space=pltpu.VMEM),
        scratch_shapes=[
            *[pltpu.VMEM((SLOTS + 1, BLK, BLK), jnp.bfloat16) for _ in SOURCES],
            pltpu.SMEM(slot_rows.shape, jnp.int32),
            pltpu.SMEM(slot_cols.shape, jnp.int32),
            pltpu.SMEM(col_window.shape, jnp.int32),
            pltpu.VMEM((COLS, 8, 128), jnp.int32),
            pltpu.SMEM((COLS, 8, 128), jnp.int32),
            pltpu.SMEM((8, 128), jnp.int32),
            pltpu.VMEM((4, BLK, BLK), jnp.bfloat16),
            pltpu.VMEM((3, BLK, BLK), jnp.bfloat16),
            pltpu.VMEM((BLK, BLK), jnp.bfloat16),
            pltpu.VMEM((8, 4, BLK, BLK), jnp.bfloat16),
            dma((28,)), dma((28,)), dma((7,)), dma((7,)), dma((7,)), dma((1,)), dma((3,)), dma((3,)),
            dma((1,)), dma((1,)), dma((19,)), dma((19,)), dma((6,)),
        ],
        compiler_params=pltpu.CompilerParams(
            collective_id=0, has_side_effects=True, vmem_limit_bytes=24 * 1024 * 1024
        ),
        cost_estimate=pl.CostEstimate(flops=2 * RL * BLK * 2048 * 256, bytes_accessed=8 * 1024 * 1024, transcendentals=0),
    )(*operands, counts)


def solution(mesh):
    placed = (
        P("row", "col", None, None, None),
        P("row", "col", None),
        P("row", "col", None),
        P("row", "col"),
        P("col", None),
    )
    return jax.shard_map(
        per_device, mesh=mesh, in_specs=placed, out_specs=P("row", "col", None, None), check_vma=False
    )
```
